32 devices in a mesh: vox: 8 (over y, x, core), load: 4 (over z).
Axes of the slice: x: 2, y: 2, z: 4, core: 2. Of those that a mesh axis runs over, the one named last changes fastest.
Arguments:
- reduced_shape_matrix: bfloat16 [8192, 512], P('vox'), may hold values from -0.25 to 0.25
- young_modulus: float32 [8192], P('vox'), may hold values from 0.5 to 2
- work_stiffening_modulus: float32 [8192], P('vox'), may hold values from 0.2 to 2
- entry_flow_stress: float32 [8192], P('vox'), may hold values from 0.5 to 2
- dilation_factor: float32 [8192], P('vox'), may hold values from 0.5 to 2
- heat_difference: float32 [512], P('load'), may hold values from -4 to 4
- flowing_entry_flags: int32 [8192, 512], P('vox', 'load'), may hold values 0 or 1
- starting_permanent_deformation: float32 [8192, 512], P('vox', 'load'), may hold values from -3 to 3
- starting_weights: float32 [512, 512], P('vox', 'load'), may hold values from -5 to 5
- applied_reduced_vector: float32 [512, 512], P('vox', 'load'), may hold values from -96 to 96
- approx_tangent_inverse: float32 [512, 512], replicated, as said below
Outputs:
- final_mode_coefficients: float32 [512, 512], P('vox', 'load')
- strain_out: float32 [8192, 512], P('vox', 'load')
The draws below stay inside these ranges and needn't reach their ends.
Inputs may be any that keep to these rules, and one draw needn't show every extreme that they name: `approx_tangent_inverse`: it has a positive diagonal.
All inputs are finite; a program needn't handle non-finite values. No bound on the sum of `flowing_entry_flags` on one device may be relied on, other than what follows from the above.
Results may differ from the reference program's by a relative error of at most 0.0013.
Values may be sent and summed in bfloat16 or wider, within the bound.
A program may use at most 64 MiB of HBM per device.

```python
import math
import jax
import jax.numpy as jnp
from jax import lax

M = 512
ITERS = 3
ROWS = 8192
NUM_HEAT_STEPS = 512


def draw_approx_tangent_inverse(key, part):
    diagonal_random_key, key_off = jax.random.split(jax.random.fold_in(key, 7))
    diag_vals = jnp.exp(jax.random.uniform(diagonal_random_key, (M,), jnp.float32, jnp.log(0.3), jnp.log(0.8)))
    offdiag = jax.random.normal(key_off, (M, M), jnp.float32) * (0.15 / jnp.sqrt(jnp.float32(M)))
    matrix = offdiag + jnp.diag(diag_vals)
    return (matrix * (M / ROWS)).astype(jnp.float32)


def plant(result, key, smallest, top_value):
    shape = result.shape
    index_at = [jax.random.randint(jax.random.fold_in(key, axis), (), 0, shape[axis]) for axis in range(len(shape))]
    result = result.at[tuple(index_at)].set(smallest)
    longest = shape.index(max(shape))
    index_at[longest] = (index_at[longest] + 1) % shape[longest]
    return result.at[tuple(index_at)].set(top_value)


def steps_of(stream_key, extent, cuts, least, high):
    def one(dim, shards_of):
        draws = jax.random.uniform(jax.random.fold_in(jax.random.fold_in(stream_key, 6), dim), (shards_of,), jnp.float32, least / len(cuts), high / len(cuts))
        return jnp.repeat(jnp.exp(draws), extent[dim] // shards_of).reshape((-1,) + (1,) * (len(extent) - dim - 1))

    loudness = one(*cuts[0])
    for cut in cuts[1:]:
        loudness = loudness * one(*cut)
    return loudness


def bell_draw(stream_key, dims, scale, most, cuts=(), kind=jnp.bfloat16):
    values = scale * jax.random.normal(stream_key, dims, jnp.float32)
    if cuts:
        values = values * steps_of(stream_key, dims, cuts, -0.22, 0.18)
    return jnp.clip(values, -most, most).astype(kind)


def setup_inputs(seed: int = 0) -> dict:
    arg_keys = jax.random.split(jax.random.key(seed), 12)
    reduced_shape_matrix = bell_draw(arg_keys[0], (ROWS, M), M ** -0.5, 0.25, ((0, 8),))
    young_modulus = jnp.clip(jnp.exp(math.log(2.0) - 1.3862944 * jax.random.uniform(arg_keys[1], (ROWS,), jnp.float32) ** steps_of(arg_keys[1], (ROWS,), ((0, 8),), -0.2, 0.2)), 0.5, 2.0)
    work_stiffening_modulus = jnp.clip(jnp.exp(math.log(2.0) - 2.3025851 * jax.random.uniform(arg_keys[2], (ROWS,), jnp.float32) ** steps_of(arg_keys[2], (ROWS,), ((0, 8),), -0.2, 0.2)), 0.2, 2.0)
    entry_flow_stress = jnp.clip(jnp.exp(math.log(2.0) - 1.3862944 * jax.random.uniform(arg_keys[3], (ROWS,), jnp.float32) ** steps_of(arg_keys[3], (ROWS,), ((0, 8),), -0.2, 0.2)), 0.5, 2.0)
    dilation_factor = jnp.clip(jnp.exp(math.log(2.0) - 1.3862944 * jax.random.uniform(arg_keys[4], (ROWS,), jnp.float32) ** steps_of(arg_keys[4], (ROWS,), ((0, 8),), -0.2, 0.2)), 0.5, 2.0)
    heat_difference = bell_draw(arg_keys[5], (NUM_HEAT_STEPS,), 1.0, 4.0, ((0, 4),), jnp.float32)
    flowing_entry_flags = plant((jax.random.randint(arg_keys[6], (ROWS, NUM_HEAT_STEPS), 0, 2) < 1).astype(jnp.int32), jax.random.fold_in(arg_keys[6], 1), 0, 1)
    starting_permanent_deformation = bell_draw(arg_keys[7], (ROWS, NUM_HEAT_STEPS), 0.5, 3.0, ((0, 8), (1, 4)), jnp.float32)
    starting_weights = bell_draw(arg_keys[8], (M, NUM_HEAT_STEPS), 1.0, 5.0, ((0, 8), (1, 4)), jnp.float32)
    applied_reduced_vector = bell_draw(arg_keys[9], (M, NUM_HEAT_STEPS), (ROWS // M), 96.0, ((0, 8), (1, 4)), jnp.float32)
    approx_tangent_inverse = draw_approx_tangent_inverse(jax.random.fold_in(arg_keys[11], 71), 0)
    return {"reduced_shape_matrix": reduced_shape_matrix, "young_modulus": young_modulus, "work_stiffening_modulus": work_stiffening_modulus, "entry_flow_stress": entry_flow_stress, "dilation_factor": dilation_factor, "heat_difference": heat_difference, "flowing_entry_flags": flowing_entry_flags, "starting_permanent_deformation": starting_permanent_deformation, "starting_weights": starting_weights, "applied_reduced_vector": applied_reduced_vector, "approx_tangent_inverse": approx_tangent_inverse}


def reference(reduced_shape_matrix, young_modulus, work_stiffening_modulus, entry_flow_stress, dilation_factor, heat_difference, flowing_entry_flags, starting_permanent_deformation, starting_weights, applied_reduced_vector, approx_tangent_inverse):
    xi_now = starting_weights
    plastic = starting_permanent_deformation
    active = flowing_entry_flags.astype(jnp.float32)
    modulus = young_modulus[:, None]
    harden = work_stiffening_modulus[:, None]
    yielded = entry_flow_stress[:, None]
    heating_history = dilation_factor[:, None] * heat_difference[None, :]
    for sweep in range(ITERS):
        strain = jnp.dot(reduced_shape_matrix, xi_now.astype(jnp.bfloat16), preferred_element_type=jnp.float32)
        trial = modulus * (strain - heating_history - plastic)
        excess = trial - yielded * jnp.tanh(trial / yielded)
        increment = active * excess / (modulus + harden)
        plastic = plastic + increment
        stress = (trial - modulus * increment).astype(jnp.bfloat16)
        resid = lax.dot_general(reduced_shape_matrix, stress, (((0,), (0,)), ((), ())), preferred_element_type=jnp.float32) - applied_reduced_vector
        delta = jnp.dot(approx_tangent_inverse, resid, precision=lax.Precision.HIGHEST)
        spread = jnp.sum(delta * delta) / (M * NUM_HEAT_STEPS)
        xi_now = xi_now - delta / (1.0 + spread)
    return xi_now, plastic
```

```python
import functools

import jax
import jax.numpy as jnp
from jax import lax
from jax.experimental import pallas as pl
from jax.experimental.pallas import tpu as pltpu
from jax.sharding import PartitionSpec as P

ITERS = 3
LANES = 128
MESH = pl.DeviceIdType.MESH
F32, BF16 = jnp.float32, jnp.bfloat16
NN = (((1,), (0,)), ((), ()))


def dot(a, b):
    return lax.dot_general(a, b, NN, preferred_element_type=F32)


def newton(
    n, nl, iters,
    a_hbm, young_ref, work_ref, flow_ref, dil_ref, heat_ref, flags_hbm, start_hbm, xi_ref, applied_ref, t_hbm,
    xi_out, plastic_out,
    a_s, t_s, flags_s, q_s, e_s, y_s, yinv_s, c_s, heat_s, t_hi, t_lo,
    xi_g, app_s, app_t, xi_t, xib, s_t, part, precv, dbuf, dlast_src, dlast, turn, zbuf, cbuf,
    load_sem, xi_send, xi_recv, p_send, p_recv, d_send, d_recv, z_send, z_recv, c_send, c_recv,
):
    me, my_load = lax.axis_index("vox"), lax.axis_index("load")
    rows, modes = a_s.shape
    own, points = xi_ref.shape
    per = points // n

    def to(k):
        return lax.rem(me + k, n)

    def fro(k):
        return lax.rem(me + n - k, n)

    def z_to(k):
        return lax.rem(my_load + k, nl)

    def z_fro(k):
        return lax.rem(my_load + nl - k, nl)

    def lane_of(j):
        return pl.multiple_of(j * own // LANES * LANES, LANES)

    def send(src, dst, send_sem, recv_sem, axis, target):
        return pltpu.make_async_remote_copy(
            src_ref=src, dst_ref=dst, send_sem=send_sem, recv_sem=recv_sem,
            device_id={axis: target}, device_id_type=MESH,
        )

    barrier = pltpu.get_barrier_semaphore()
    for k in range(1, n):
        pl.semaphore_signal(barrier, inc=1, device_id={"vox": to(k)}, device_id_type=MESH)
    for k in range(1, nl):
        pl.semaphore_signal(barrier, inc=1, device_id={"load": z_to(k)}, device_id_type=MESH)
    loads = [
        pltpu.make_async_copy(s, d, load_sem.at[i])
        for i, (s, d) in enumerate(((flags_hbm, flags_s), (start_hbm, q_s), (t_hbm, t_s), (a_hbm, a_s)))
    ]
    for c in loads:
        c.start()
    pl.semaphore_wait(barrier, n + nl - 2)

    xi_sends = [
        send(xi_ref, xi_g.at[me], xi_send.at[k - 1], xi_recv.at[k - 1], "vox", to(k)) for k in range(1, n)
    ]
    for c in xi_sends:
        c.start()
    xi_g[me] = xi_ref[...]

    for c in loads[:2]:
        c.wait()
    count = rows // LANES
    stack = [young_ref[...], work_ref[...], flow_ref[...], dil_ref[...]]
    packed = jnp.concatenate(stack + [jnp.zeros((LANES - 4 * count, LANES), F32)], axis=0).T
    for i in range(count):
        at = pl.ds(i * LANES, LANES)
        young, work, flow, dil = (
            jnp.broadcast_to(packed[:, p * count + i : p * count + i + 1], (LANES, points)) for p in range(4)
        )
        warm = dil * heat_ref[...]
        e_s[at, :] = young
        y_s[at, :] = flow
        yinv_s[at, :] = 1.0 / flow
        c_s[at, :] = flags_s[at, :].astype(F32) / (young + work)
        heat_s[at, :] = warm
        q_s[at, :] = q_s[at, :] + warm
    app_s[...] = jnp.zeros_like(app_s)
    app_s[me] = applied_ref[...]
    app_t[...] = app_s[...].reshape(modes, points).T
    loads[2].wait()
    for i in range(modes // LANES):
        at = pl.ds(i * LANES, LANES)
        block = t_s[at, :].T
        high = block.astype(BF16)
        t_hi[:, at] = high
        t_lo[:, at] = (block - high.astype(F32)).astype(BF16)
    loads[3].wait()

    for k in range(1, n):
        send(xi_ref, xi_g.at[fro(k)], xi_send.at[k - 1], xi_recv.at[k - 1], "vox", to(k)).wait_recv()
    xib[...] = xi_g[...].reshape(modes, points).astype(BF16)

    chunk = 256
    for it in range(iters):
        final = it == iters - 1
        for i in range(rows // chunk):
            at = pl.ds(i * chunk, chunk)
            e, q = e_s[at, :], q_s[at, :]
            trial = e * (dot(a_s[at, :], xib[...]) - q)
            excess = trial - y_s[at, :] * jnp.tanh(trial * yinv_s[at, :])
            increment = c_s[at, :] * excess
            q = q + increment
            if final:
                plastic_out[at, :] = q - heat_s[at, :]
            else:
                q_s[at, :] = q
            s_t[:, at] = (trial - e * increment).astype(BF16).T
        if it > 0:
            for c in p_copies:
                c.wait_send()
        part[...] = (dot(s_t[...], a_s[...]) - app_t[...]).reshape(n, per, modes)

        p_copies = [
            send(part.at[to(k)], precv.at[it, k - 1], p_send.at[it, k - 1], p_recv.at[it, k - 1], "vox", to(k))
            for k in range(1, n)
        ]
        for c in p_copies:
            c.start()
        if it == 0:
            for c in xi_sends:
                c.wait_send()
            xi_t[...] = xi_g[...].reshape(modes, points).T
        resid = part[me]
        for k in range(1, n):
            p_copies[k - 1].wait_recv()
            resid = resid + precv[it, k - 1]
        r_hi = resid.astype(BF16)
        r_lo = (resid - r_hi.astype(F32)).astype(BF16)
        both = dot(jnp.concatenate([r_hi, r_lo], axis=0), t_hi[...])
        delta = both[:per] + (both[per:] + dot(r_hi, t_lo[...]))

        square = delta * delta
        tile = jnp.sum(square.reshape(per // 8, 8, modes), axis=0)
        zbuf[it, my_load] = sum(tile[:, j * LANES : (j + 1) * LANES] for j in range(modes // LANES))
        z_copies = [
            send(zbuf.at[it, my_load], zbuf.at[it, my_load], z_send.at[it, k - 1], z_recv.at[it, k - 1], "load", z_to(k))
            for k in range(1, nl)
        ]
        for c in z_copies:
            c.start()
        if final:
            dlast_src[...] = delta
            dlast[me] = dlast_src[:, pl.ds(lane_of(me), LANES)]
            d_copies = [
                send(
                    dlast_src.at[:, pl.ds(lane_of(to(k)), LANES)], dlast.at[me],
                    d_send.at[it, k - 1], d_recv.at[it, k - 1], "vox", to(k),
                )
                for k in range(1, n)
            ]
        else:
            dbuf[it, me] = delta
            d_copies = [
                send(dbuf.at[it, me], dbuf.at[it, me], d_send.at[it, k - 1], d_recv.at[it, k - 1], "vox", to(k))
                for k in range(1, n)
            ]
        for c in d_copies:
            c.start()
        for k in range(1, nl):
            send(
                zbuf.at[it, my_load], zbuf.at[it, z_fro(k)], z_send.at[it, k - 1], z_recv.at[it, k - 1], "load", z_to(k)
            ).wait_recv()
        cbuf[it, me] = jnp.sum(zbuf[it], axis=0)
        c_copies = [
            send(cbuf.at[it, me], cbuf.at[it, me], c_send.at[it, k - 1], c_recv.at[it, k - 1], "vox", to(k))
            for k in range(1, n)
        ]
        for c in c_copies:
            c.start()
        for k in range(1, n):
            if final:
                here = send(
                    dlast_src.at[:, pl.ds(lane_of(to(k)), LANES)], dlast.at[fro(k)],
                    d_send.at[it, k - 1], d_recv.at[it, k - 1], "vox", to(k),
                )
            else:
                here = send(
                    dbuf.at[it, me], dbuf.at[it, fro(k)], d_send.at[it, k - 1], d_recv.at[it, k - 1], "vox", to(k)
                )
            here.wait_recv()
        for k in range(1, n):
            send(
                cbuf.at[it, me], cbuf.at[it, fro(k)], c_send.at[it, k - 1], c_recv.at[it, k - 1], "vox", to(k)
            ).wait_recv()
        spread = jnp.sum(jnp.sum(cbuf[it], axis=0), keepdims=True) / (modes * points * nl)
        damp = 1.0 / (1.0 + spread)
        if final:
            last = xi_t[:, pl.ds(lane_of(me), LANES)] - dlast[...].reshape(points, LANES) * damp
            turn[...] = last.T
            xi_out[...] = turn[pl.ds(pl.multiple_of(lax.rem(me * own, LANES), own), own), :]
        else:
            now = xi_t[...] - dbuf[it].reshape(points, modes) * damp
            xi_t[...] = now
            xib[...] = now.T.astype(BF16)
        for c in z_copies + d_copies + c_copies:
            c.wait_send()
    for c in p_copies:
        c.wait_send()


def fused(n, nl, a, young, work, flow, dil, heat, flags, start, xi, applied, tangent):
    rows, modes = a.shape
    own, points = xi.shape
    per, count = points // n, rows // LANES
    as_rows = [v.reshape(count, LANES) for v in (young, work, flow, dil)]
    full = lambda dtype: pltpu.VMEM((rows, points), dtype)
    dma = lambda *shape: pltpu.SemaphoreType.DMA(shape)
    in_vmem, in_hbm = pl.BlockSpec(memory_space=pltpu.VMEM), pl.BlockSpec(memory_space=pl.ANY)
    return pl.pallas_call(
        functools.partial(newton, n, nl, ITERS),
        out_shape=(jax.ShapeDtypeStruct((own, points), F32), jax.ShapeDtypeStruct((rows, points), F32)),
        in_specs=[in_hbm] + [in_vmem] * 5 + [in_hbm] * 2 + [in_vmem] * 2 + [in_hbm],
        out_specs=(in_vmem, in_vmem),
        scratch_shapes=[
            pltpu.VMEM((rows, modes), BF16), pltpu.VMEM((modes, modes), F32), full(jnp.int32),
            full(F32), full(F32), full(F32), full(F32), full(F32), full(F32),
            pltpu.VMEM((modes, modes), BF16), pltpu.VMEM((modes, modes), BF16),
            pltpu.VMEM((n, own, points), F32), pltpu.VMEM((n, own, points), F32),
            pltpu.VMEM((points, modes), F32), pltpu.VMEM((points, modes), F32),
            pltpu.VMEM((modes, points), BF16), pltpu.VMEM((points, rows), BF16),
            pltpu.VMEM((n, per, modes), F32), pltpu.VMEM((ITERS, n - 1, per, modes), F32),
            pltpu.VMEM((ITERS - 1, n, per, modes), F32), pltpu.VMEM((per, modes), F32),
            pltpu.VMEM((n, per, LANES), F32), pltpu.VMEM((LANES, points), F32),
            pltpu.VMEM((ITERS, nl, 8, LANES), F32), pltpu.VMEM((ITERS, n, 8, LANES), F32),
            dma(4), dma(n - 1), dma(n - 1), dma(ITERS, n - 1), dma(ITERS, n - 1), dma(ITERS, n - 1),
            dma(ITERS, n - 1), dma(ITERS, nl - 1), dma(ITERS, nl - 1), dma(ITERS, n - 1), dma(ITERS, n - 1),
        ],
        compiler_params=pltpu.CompilerParams(
            collective_id=0, has_side_effects=True, vmem_limit_bytes=40 * 1024 * 1024
        ),
    )(a, *as_rows, heat.reshape(1, points), flags, start, xi, applied, tangent)


def fits(n, nl, a, xi):
    (rows, modes), (own, points) = a.shape, xi.shape
    return (
        n > 1 and nl > 1 and rows % 256 == 0 and 4 * rows <= LANES * LANES and modes % LANES == 0
        and points == LANES and points % (8 * n) == 0 and own % 8 == 0 and LANES % own == 0
    )


def plain(
    reduced_shape_matrix,
    young_modulus,
    work_stiffening_modulus,
    entry_flow_stress,
    dilation_factor,
    heat_difference,
    flowing_entry_flags,
    starting_permanent_deformation,
    starting_weights,
    applied_reduced_vector,
    approx_tangent_inverse,
):
    own_rows = starting_weights.shape[0]
    points = starting_weights.shape[1]
    load_point_total = points * lax.axis_size("load")
    plastic = starting_permanent_deformation
    active = flowing_entry_flags.astype(jnp.float32)
    modulus = young_modulus[:, None]
    harden = work_stiffening_modulus[:, None]
    yielded = entry_flow_stress[:, None]
    heating_history = dilation_factor[:, None] * heat_difference[None, :]
    xi_now, force_all = (
        lax.all_gather(starting_weights, "vox", axis=0, tiled=True),
        lax.all_gather(applied_reduced_vector, "vox", axis=0, tiled=True),
    )
    for sweep in range(ITERS):
        strain = jnp.dot(
            reduced_shape_matrix, xi_now.astype(jnp.bfloat16), preferred_element_type=jnp.float32
        )
        trial = modulus * (strain - heating_history - plastic)
        excess = trial - yielded * jnp.tanh(trial / yielded)
        increment = active * excess / (modulus + harden)
        stress = (trial - modulus * increment).astype(jnp.bfloat16)
        stress, plastic = (stress, plastic + increment)
        partial_sum = lax.dot_general(
            reduced_shape_matrix,
            stress,
            (((0,), (0,)), ((), ())),
            preferred_element_type=jnp.float32,
        )
        resid = lax.psum(partial_sum, "vox") - force_all
        delta = jnp.dot(approx_tangent_inverse, resid, precision=lax.Precision.HIGHEST)
        spread = lax.psum(jnp.sum(delta * delta), "load") / (starting_weights.shape[0] * lax.axis_size("vox") * load_point_total)
        xi_now = xi_now - delta / (1.0 + spread)
    mine = lax.dynamic_slice_in_dim(xi_now, lax.axis_index("vox") * own_rows, own_rows, 0)
    return (mine, plastic)


def shards(*args):
    n, nl = lax.axis_size("vox"), lax.axis_size("load")
    if fits(n, nl, args[0], args[8]):
        return fused(n, nl, *args)
    return plain(*args)


def solution(mesh):
    in_specs = (
        P("vox", None),
        P("vox"),
        P("vox"),
        P("vox"),
        P("vox"),
        P("load"),
        P("vox", "load"),
        P("vox", "load"),
        P("vox", "load"),
        P("vox", "load"),
        P(),
    )
    out_specs = (P("vox", "load"), P("vox", "load"))
    return jax.shard_map(shards, mesh=mesh, in_specs=in_specs, out_specs=out_specs, check_vma=False)
```
